32 devices in a mesh: blk: 8 (over z, x), cols: 4 (over y, core).
Axes of the slice: x: 2, y: 2, z: 4, core: 2. Of those that a mesh axis runs over, the one named last changes fastest.
Arguments:
- focusing_plus: float32 [9728, 16, 512], P(('cols', 'blk')), may hold values from -6 to 6
- direct_field: float32 [9728, 16, 512], P(('cols', 'blk')), may hold values from -4 to 4
- reflectivity: float32 [2, 2, 9728, 9728], P(None, None, 'blk', 'cols'), may hold values from -0.0625 to 0.0625
- frequency_bins: int32 [2], replicated, may hold values from 64 to 247
- focal_onsets: int32 [16], replicated, may hold values from 32 to 191
- line_offsets: int32 [128], replicated, may hold values from 0 to 63
Outputs:
- focusing_update: float32 [9728, 16, 512], P(('cols', 'blk'))
The draws below stay inside these ranges and needn't reach their ends.
All inputs are finite; a program needn't handle non-finite values.
Results may differ from the reference program's by a relative error of at most 0.000092.
Values sent between devices are 32-bit elements; how exact they have to be, the bound alone decides.
A program may use at most 128 MiB of HBM per device.

```python
import math
import jax
import jax.numpy as jnp
from jax import lax

ORDER = 9728
NT = 512
NW = 2
NF = 16
LINE = 76
LINES = 128


def set_ends(array, rng, least, largest):
    shape = array.shape
    spot = [jax.random.randint(jax.random.fold_in(rng, axis), (), 0, shape[axis]) for axis in range(len(shape))]
    array = array.at[tuple(spot)].set(least)
    longest = shape.index(max(shape))
    spot[longest] = (spot[longest] + 1) % shape[longest]
    return array.at[tuple(spot)].set(largest)


def block_scale(key, extent, split, smallest, high):
    factor_of, own = 1.0, jax.random.fold_in(key, 6)
    for dim, blocks in split:
        heights = jnp.exp(jax.random.uniform(jax.random.fold_in(own, dim), (blocks,), jnp.float32, smallest / len(split), high / len(split)))
        factor_of = factor_of * jnp.repeat(heights, extent[dim] // blocks).reshape([-1 if axis == dim else 1 for axis in range(len(extent))])
    return factor_of


def centred(key, shape, deviation, reach, split=(), kind=jnp.bfloat16):
    values = deviation * jax.random.normal(key, shape, jnp.float32)
    if split:
        values = values * block_scale(key, shape, split, -0.22, 0.18)
    return jnp.clip(values, -reach, reach).astype(kind)


def setup_inputs(seed: int = 0) -> dict:
    splits = jax.random.split(jax.random.key(seed), 7)
    return {
        "focusing_plus": centred(splits[0], (ORDER, NF, NT), 1.0, 6.0, ((0, 32),), jnp.float32),
        "direct_field": centred(splits[1], (ORDER, NF, NT), 0.5, 4.0, ((0, 32),), jnp.float32),
        "reflectivity": centred(splits[2], (NW, 2, ORDER, ORDER), ORDER ** -0.5, 0.0625, ((2, 8), (3, 4)), jnp.float32),
        "frequency_bins": jax.random.randint(splits[3], (NW,), NT // 8, NT // 2 - 8).astype(jnp.int32),
        "focal_onsets": set_ends(jax.random.randint(splits[4], (NF,), NT // 16, 3 * NT // 8), jax.random.fold_in(splits[4], 1), NT // 16, (3 * NT // 8) - 1).astype(jnp.int32),
        "line_offsets": set_ends(jax.random.randint(splits[5], (LINES,), 0, NT // 8), jax.random.fold_in(splits[5], 1), 0, (NT // 8) - 1).astype(jnp.int32),
    }


highest = lax.Precision.HIGHEST

def wave_tables(frequency_bins, samples):
    times = jnp.arange(samples, dtype=jnp.int32)
    phases = frequency_bins[:, None] * times[None, :] % samples
    angles = phases.astype(jnp.float32) * (2.0 * math.pi / samples)
    inverse = jnp.stack([jnp.cos(angles), -jnp.sin(angles)], axis=1).reshape(-1, samples)
    forward = inverse / math.sqrt(samples)
    return (forward, inverse)

def to_spectrum(signal, forward):
    positions, focal, samples = signal.shape
    flat = signal.reshape(positions * focal, samples)
    result = lax.dot_general(forward, flat, (((1,), (1,)), ((), ())), precision=highest, preferred_element_type=jnp.float32)
    return result.reshape(-1, 2, positions, focal)

def to_signal(spectrum, inverse):
    waves, halves, positions, focal = spectrum.shape
    flat = spectrum.reshape(waves * halves, positions * focal)
    result = lax.dot_general(flat, inverse, (((0,), (0,)), ((), ())), precision=highest, preferred_element_type=jnp.float32)
    return result.reshape(positions, focal, -1)

def apply_window(signal, first_row, focal_onsets, line_offsets, line_length):
    positions, focal, samples = signal.shape
    lines = lax.dynamic_slice_in_dim(line_offsets, (first_row // line_length).astype(jnp.int32), positions // line_length)
    per_row = jnp.repeat(lines, line_length)
    onsets = focal_onsets[None, :] + per_row[:, None]
    times = jnp.arange(samples, dtype=jnp.int32)
    window = (times[None, None, :] < onsets[:, :, None]) | (times[None, None, :] >= samples - onsets[:, :, None])
    return jnp.where(window, signal, jnp.zeros_like(signal))

def kernel_apply(kernel, spectrum):
    parts = jnp.einsum('wprs,wqsf->wpqrf', kernel, spectrum, precision=highest)
    real = parts[:, 0, 0] - parts[:, 1, 1]
    imag = parts[:, 0, 1] + parts[:, 1, 0]
    return jnp.stack([real, imag], axis=1)

def kernel_adjoint(kernel, spectrum):
    parts = jnp.einsum('wprs,wqrf->wpqsf', kernel, spectrum, precision=highest)
    real = parts[:, 0, 0] + parts[:, 1, 1]
    imag = parts[:, 0, 1] - parts[:, 1, 0]
    return jnp.stack([real, imag], axis=1)

def reference(focusing_plus, direct_field, reflectivity, frequency_bins, focal_onsets, line_offsets):
    samples = focusing_plus.shape[2]
    forward, inverse = wave_tables(frequency_bins, samples)
    anchor = jnp.zeros((), jnp.int32)
    plus_spectrum = to_spectrum(focusing_plus, forward)
    upgoing = kernel_apply(reflectivity, plus_spectrum)
    focusing_minus = apply_window(to_signal(upgoing, inverse), anchor, focal_onsets, line_offsets, LINE)
    minus_spectrum = to_spectrum(focusing_minus, forward)
    adjoint = kernel_adjoint(reflectivity, minus_spectrum)
    correction = apply_window(to_signal(adjoint, inverse), anchor, focal_onsets, line_offsets, LINE)
    return direct_field - correction
```

```python
import math

import jax
import jax.numpy as jnp
from jax import lax
from jax.sharding import PartitionSpec as P

LINE = 76


high = lax.Precision.HIGH
highest = lax.Precision.HIGHEST


def wave_tables(frequency_bins, samples):
    times = jnp.arange(samples, dtype=jnp.int32)
    phases = frequency_bins[:, None] * times[None, :] % samples
    angles = phases.astype(jnp.float32) * (2.0 * math.pi / samples)
    inverse = jnp.stack([jnp.cos(angles), -jnp.sin(angles)], axis=1).reshape(-1, samples)
    forward = inverse / math.sqrt(samples)
    return (forward, inverse)


def windows(first_row, positions, focal_onsets, line_offsets, samples):
    lines = lax.dynamic_slice_in_dim(line_offsets, first_row // LINE, positions // LINE)
    onsets = (focal_onsets[:, None] + lines[None, :])[:, :, None]
    times = jnp.arange(samples, dtype=jnp.int32)
    return (times < onsets) | (times >= samples - onsets)


def local(focusing_plus, direct_field, reflectivity, frequency_bins, focal_onsets, line_offsets):
    own, focal, samples = focusing_plus.shape
    waves, _, block_rows, group_columns = reflectivity.shape
    forward, inverse = wave_tables(frequency_bins, samples)
    block_index = lax.axis_index("blk")
    group_index = lax.axis_index("cols")
    rows = 2 * waves * focal

    spectrum = lax.dot_general(
        forward, focusing_plus.reshape(own * focal, samples), (((1,), (1,)), ((), ())),
        precision=high, preferred_element_type=jnp.float32,
    )
    spectrum = spectrum.reshape(-1, own, focal).transpose(0, 2, 1).reshape(rows, own)
    gathered = lax.all_gather(spectrum, "blk", axis=0).transpose(1, 0, 2)
    gathered = gathered.reshape(waves, 2, focal, group_columns)
    real, imag = gathered[:, 0], gathered[:, 1]
    left = jnp.stack(
        [jnp.concatenate([real, imag], 1), jnp.concatenate([-imag, real], 1)], axis=1
    )
    partial_up = jnp.einsum("wpns,wprs->wnr", left, reflectivity, precision=high)
    groups = block_rows // own
    partial_up = partial_up.reshape(rows, groups, own).transpose(1, 0, 2)
    share = lax.psum_scatter(partial_up, "cols", scatter_dimension=0)

    first_share = block_index * block_rows + group_index * own
    window = windows(first_share, own, focal_onsets, line_offsets, samples)
    mix = jnp.einsum(
        "flt,kjt->kjfl", window.astype(jnp.float32), forward[:, None] * inverse[None],
        precision=highest,
    )
    mix = jnp.repeat(mix, LINE, axis=3)
    share = share.reshape(2 * waves, focal, own)
    minus = (mix * share[None]).sum(axis=1).reshape(rows, own)

    minus = lax.all_gather(minus, "cols", axis=0).transpose(1, 0, 2)
    minus = minus.reshape(waves, 2, focal, block_rows)
    real, imag = minus[:, 0], minus[:, 1]
    left = jnp.stack(
        [jnp.concatenate([real, imag], 1), jnp.concatenate([imag, -real], 1)], axis=1
    )
    partial_adj = jnp.einsum("wpnr,wprs->wns", left, reflectivity, precision=high)
    partial_adj = partial_adj.reshape(rows, group_columns // own, own).transpose(1, 0, 2)
    update = lax.psum_scatter(partial_adj, "blk", scatter_dimension=0)

    first_source = group_index * group_columns + block_index * own
    window = windows(first_source, own, focal_onsets, line_offsets, samples)
    window = jnp.repeat(window.transpose(1, 0, 2), LINE, axis=0)
    update = update.reshape(2 * waves, focal, own).transpose(0, 2, 1).reshape(2 * waves, -1)
    correction = lax.dot_general(
        update, inverse, (((0,), (0,)), ((), ())),
        precision=high, preferred_element_type=jnp.float32,
    ).reshape(own, focal, samples)
    return direct_field - jnp.where(window, correction, jnp.zeros_like(correction))


def solution(mesh):
    return jax.shard_map(
        local,
        mesh=mesh,
        in_specs=(
            P(("cols", "blk"), None, None),
            P(("cols", "blk"), None, None),
            P(None, None, "blk", "cols"),
            P(),
            P(),
            P(),
        ),
        out_specs=P(("cols", "blk"), None, None),
        check_vma=False,
    )
```

```python
import functools
import math

import jax
import jax.numpy as jnp
from jax import lax
from jax.experimental import pallas as pl
from jax.experimental.pallas import tpu as pltpu
from jax.sharding import PartitionSpec as P

LINE = 76
MESH = pl.DeviceIdType.MESH
F32 = jnp.float32
BF16 = jnp.bfloat16


high = lax.Precision.HIGH
highest = lax.Precision.HIGHEST


def wave_tables(frequency_bins, samples):
    times = jnp.arange(samples, dtype=jnp.int32)
    phases = frequency_bins[:, None] * times[None, :] % samples
    angles = phases.astype(jnp.float32) * (2.0 * math.pi / samples)
    inverse = jnp.stack([jnp.cos(angles), -jnp.sin(angles)], axis=1).reshape(-1, samples)
    forward = inverse / math.sqrt(samples)
    return (forward, inverse)


def windows(first_row, positions, focal_onsets, line_offsets, samples):
    lines = lax.dynamic_slice_in_dim(line_offsets, first_row // LINE, positions // LINE)
    onsets = (focal_onsets[:, None] + lines[None, :])[:, :, None]
    times = jnp.arange(samples, dtype=jnp.int32)
    return (times < onsets) | (times >= samples - onsets)


def split(value):
    upper = value.astype(BF16).astype(F32)
    return upper, value - upper


def pieces_of(columns):
    width = 512
    starts = list(range(0, columns, width))
    order = []
    while starts:
        order.append(starts.pop(0))
        if starts:
            order.append(starts.pop())
    return [(start, min(width, columns - start)) for start in order]


def kernel(
    nb, nc, focal, waves, block_rows, group_columns, own, chunk,
    x_hbm, k_hbm, fwd_ref, mix_ref, out_ref,
    xbuf, stage, upper, lower, spec, ag, table, wide, right, up_send, up_recv, mins, left, adj_recv,
    x_sem, k_sem, ag_s, ag_r, up_s, up_r, mi_s, mi_r, ad_s, ad_r,
):
    b = lax.axis_index("blk")
    c = lax.axis_index("cols")
    lines = own // LINE
    lane_tiles = xbuf.shape[1]
    half = 2 * focal
    rows = waves * half
    slots, room = stage.shape[0], xbuf.shape[0]
    chunks = k_hbm.shape[0] // chunk

    def x_copy(line, tile):
        return pltpu.make_async_copy(
            x_hbm.at[pl.ds(line * LINE * focal, LINE * focal), pl.ds(tile * 128, 128)],
            xbuf.at[line % room, tile], x_sem.at[line % room, tile],
        )

    def k_copy(index, slot):
        return pltpu.make_async_copy(
            k_hbm.at[pl.ds(pl.multiple_of(index * chunk, chunk), chunk)],
            stage.at[slot], k_sem.at[slot],
        )

    def to_blk(other):
        return {"blk": other}

    def to_cols(other):
        return {"cols": other}

    for line in range(room):
        for tile in range(lane_tiles):
            x_copy(line, tile).start()
    for slot in range(slots):
        k_copy(slot, slot).start()

    barrier = pltpu.get_barrier_semaphore()
    for d in range(1, nb):
        pl.semaphore_signal(barrier, inc=1, device_id=to_blk(lax.rem(b + d, nb)), device_id_type=MESH)
    for d in range(1, nc):
        pl.semaphore_signal(barrier, inc=1, device_id=to_cols(lax.rem(c + d, nc)), device_id_type=MESH)
    pl.semaphore_wait(barrier, nb + nc - 2)

    fwd = jnp.concatenate(split(fwd_ref[...]), axis=0).astype(BF16)
    for line in range(lines):
        for tile in range(lane_tiles):
            x_copy(line, tile).wait()
        for f in range(focal):
            x = jnp.concatenate(
                [xbuf.at[line % room, tile][pl.ds(f, LINE, stride=focal), :] for tile in range(lane_tiles)], axis=1
            )
            x_upper = x.astype(BF16)
            x_lower = (x - x_upper.astype(F32)).astype(BF16)
            dims = (((1,), (1,)), ((), ()))
            both = lax.dot_general(fwd, x_upper, dims, preferred_element_type=F32)
            both += lax.dot_general(fwd, x_lower, dims, preferred_element_type=F32)
            both = both[: both.shape[0] // 2] + both[both.shape[0] // 2 :]
            for j in range(2 * waves):
                spec[line, j * focal + f : j * focal + f + 1, :] = both[j : j + 1, :]
        if line + room < lines:
            for tile in range(lane_tiles):
                x_copy(line + room, tile).start()
    for line in range(lines):
        ag[b, :, line * LINE : (line + 1) * LINE] = spec[line]

    def ag_copy(d):
        return pltpu.make_async_remote_copy(
            src_ref=ag.at[b], dst_ref=ag.at[b], send_sem=ag_s.at[d], recv_sem=ag_r.at[d],
            device_id=to_blk(lax.rem(b + d, nb)), device_id_type=MESH,
        )

    for d in range(1, nb):
        ag_copy(d).start()

    @pl.loop(0, chunks)
    def _(index):
        slot = lax.rem(index, slots)
        k_copy(index, slot).wait()
        value = stage[slot]
        value_upper = value.astype(BF16)
        place = pl.ds(pl.multiple_of(index * chunk, chunk), chunk)
        upper[place, :] = value_upper
        lower[place, :] = (value - value_upper.astype(F32)).astype(BF16)

        @pl.when(index + slots < chunks)
        def _():
            k_copy(index + slots, slot).start()

    for d in range(1, nb):
        ag_copy(d).wait()
    for other in range(nb):
        wide[:, other * own : (other + 1) * own] = ag[other]

    def operands(value, signs):
        out = []
        for p in range(2):
            stacked = []
            for w in range(waves):
                real = value[w * half : w * half + focal]
                imag = value[w * half + focal : (w + 1) * half]
                pair = [real, imag] if p == 0 else ([-imag, real] if signs else [imag, -real])
                stacked += list(split(jnp.concatenate(pair, axis=0)))
            out.append(jnp.concatenate(stacked, axis=0))
        return out

    for tile in range(group_columns // 128):
        place = slice(tile * 128, (tile + 1) * 128)
        for p, value in enumerate(operands(wide[:, place], True)):
            right[p, place, :] = value.T.astype(BF16)

    def forward_rows(start, count):
        found = []
        for w in range(waves):
            total = None
            for p in range(2):
                place = pl.ds((w * 2 + p) * block_rows + start, count)
                if not isinstance(start, int):
                    place = pl.ds(pl.multiple_of((w * 2 + p) * block_rows + start, 16), count)
                for part in (upper, lower):
                    term = jnp.dot(part[place, :], right[p], preferred_element_type=F32)
                    total = term if total is None else total + term
            turned = total.T
            first = turned[2 * w * half : (2 * w + 1) * half]
            found.append(first + turned[(2 * w + 1) * half : (2 * w + 2) * half])
        return found

    def up_copy(d):
        other = lax.rem(c + d, nc)
        return pltpu.make_async_remote_copy(
            src_ref=up_send.at[other], dst_ref=up_recv.at[d], send_sem=up_s.at[d], recv_sem=up_r.at[d],
            device_id=to_cols(other), device_id_type=MESH,
        )

    if own % 16 == 0:
        for d in list(range(1, nc)) + [0]:
            other = lax.rem(c + d, nc)
            for w, value in enumerate(forward_rows(other * own, own)):
                up_send[other, w * half : (w + 1) * half, :] = value
            if d:
                up_copy(d).start()
    else:
        for w, value in enumerate(forward_rows(0, block_rows)):
            for other in range(nc):
                up_send[other, w * half : (w + 1) * half, :] = value[:, other * own : (other + 1) * own]
        for d in range(1, nc):
            up_copy(d).start()
    share = up_send[c]
    for d in range(1, nc):
        up_copy(d).wait()
        share = share + up_recv[d]

    for k in range(2 * waves):
        total = None
        for j in range(2 * waves):
            at = (k * 2 * waves + j) * focal
            term = mix_ref[at : at + focal, :] * share[j * focal : (j + 1) * focal]
            total = term if total is None else total + term
        mins[c, k * focal : (k + 1) * focal, :] = total

    def mi_copy(d):
        return pltpu.make_async_remote_copy(
            src_ref=mins.at[c], dst_ref=mins.at[c], send_sem=mi_s.at[d], recv_sem=mi_r.at[d],
            device_id=to_cols(lax.rem(c + d, nc)), device_id_type=MESH,
        )

    for d in range(1, nc):
        mi_copy(d).start()
    for d in range(1, nc):
        mi_copy(d).wait()
    for other in range(nc):
        table[:, other * own : (other + 1) * own] = mins[other]
    for p, value in enumerate(operands(table[...], False)):
        left[p] = value.astype(BF16)

    def ad_copy(other):
        d = lax.rem(other - b + nb, nb)
        return pltpu.make_async_remote_copy(
            src_ref=ag.at[other], dst_ref=adj_recv.at[d], send_sem=ad_s.at[d], recv_sem=ad_r.at[d],
            device_id=to_blk(other), device_id_type=MESH,
        )

    done = [False] * group_columns
    sent = set()
    for start, width in pieces_of(group_columns):
        place = slice(start, start + width)
        for w in range(waves):
            total = None
            for p in range(2):
                lhs = left[p, 2 * w * half : (2 * w + 2) * half, :]
                span = slice((w * 2 + p) * block_rows, (w * 2 + p + 1) * block_rows)
                for part in (upper, lower):
                    term = jnp.dot(lhs, part[span, place], preferred_element_type=F32)
                    total = term if total is None else total + term
            wide[w * half : (w + 1) * half, place] = total[:half] + total[half:]
        done[start : start + width] = [True] * width
        for other in range(nb):
            if other not in sent and all(done[other * own : (other + 1) * own]):
                sent.add(other)
                ag[other] = wide[:, other * own : (other + 1) * own]

                @pl.when(b != other)
                def _(other=other):
                    ad_copy(other).start()

    total = ag[b]
    for d in range(1, nb):
        ad_copy(lax.rem(b + d, nb)).wait()
        total = total + adj_recv[d]
    out_ref[...] = total


def products(spectral, kernel_rows, fwd, mix, nb, nc, focal, waves, own):
    group_columns = kernel_rows.shape[1]
    block_rows = kernel_rows.shape[0] // (2 * waves)
    samples = spectral.shape[1]
    rows = 2 * waves * focal
    chunk = next(size for size in (64, 32, 16, 8) if kernel_rows.shape[0] % size == 0)
    lines, tiles, slots = own // LINE, samples // 128, 4
    dma = pltpu.SemaphoreType.DMA
    moved = 4 * (spectral.size + kernel_rows.size)
    return pl.pallas_call(
        functools.partial(kernel, nb, nc, focal, waves, block_rows, group_columns, own, chunk),
        out_shape=jax.ShapeDtypeStruct((rows, own), F32),
        in_specs=[pl.BlockSpec(memory_space=pl.ANY)] * 2 + [pl.BlockSpec(memory_space=pltpu.VMEM)] * 2,
        out_specs=pl.BlockSpec(memory_space=pltpu.VMEM),
        scratch_shapes=[
            pltpu.VMEM((min(lines, 3), tiles, LINE * focal, 128), F32),
            pltpu.VMEM((slots, chunk, group_columns), F32),
            pltpu.VMEM(kernel_rows.shape, BF16),
            pltpu.VMEM(kernel_rows.shape, BF16),
            pltpu.VMEM((lines, rows, LINE), F32),
            pltpu.VMEM((nb, rows, own), F32),
            pltpu.VMEM((rows, block_rows), F32),
            pltpu.VMEM((rows, group_columns), F32),
            pltpu.VMEM((2, group_columns, 2 * rows), BF16),
            pltpu.VMEM((nc, rows, own), F32),
            pltpu.VMEM((nc, rows, own), F32),
            pltpu.VMEM((nc, rows, own), F32),
            pltpu.VMEM((2, 2 * rows, block_rows), BF16),
            pltpu.VMEM((nb, rows, own), F32),
            dma((min(lines, 3), tiles)), dma((slots,)),
            dma((nb,)), dma((nb,)), dma((nc,)), dma((nc,)), dma((nc,)), dma((nc,)), dma((nb,)), dma((nb,)),
        ],
        compiler_params=pltpu.CompilerParams(
            collective_id=0, has_side_effects=True, vmem_limit_bytes=63 << 20
        ),
        cost_estimate=pl.CostEstimate(
            flops=16 * kernel_rows.size * focal, bytes_accessed=moved, transcendentals=0
        ),
    )(spectral, kernel_rows, fwd, mix)


def local(focusing_plus, direct_field, reflectivity, frequency_bins, focal_onsets, line_offsets, nb, nc):
    own, focal, samples = focusing_plus.shape
    waves, _, block_rows, group_columns = reflectivity.shape
    forward, inverse = wave_tables(frequency_bins, samples)
    block_index = lax.axis_index("blk")
    group_index = lax.axis_index("cols")

    first_share = block_index * block_rows + group_index * own
    window = windows(first_share, own, focal_onsets, line_offsets, samples)
    mix = jnp.einsum(
        "flt,kjt->kjfl", window.astype(F32), forward[:, None] * inverse[None],
        precision=highest,
    )
    mix = jnp.repeat(mix, LINE, axis=3).reshape(-1, own)
    fwd = jnp.pad(forward, ((0, 8 - 2 * waves), (0, 0)))
    update = products(
        focusing_plus.reshape(own * focal, samples), reflectivity.reshape(-1, group_columns),
        fwd, mix, nb, nc, focal, waves, own,
    )

    first_source = group_index * group_columns + block_index * own
    window = windows(first_source, own, focal_onsets, line_offsets, samples)
    window = jnp.repeat(window.transpose(1, 0, 2), LINE, axis=0)
    update = update.reshape(2 * waves, focal, own).transpose(0, 2, 1).reshape(2 * waves, -1)
    correction = lax.dot_general(
        update, inverse, (((0,), (0,)), ((), ())),
        precision=high, preferred_element_type=jnp.float32,
    ).reshape(own, focal, samples)
    return direct_field - jnp.where(window, correction, jnp.zeros_like(correction))


def solution(mesh):
    nb, nc = mesh.shape["blk"], mesh.shape["cols"]
    return jax.shard_map(
        functools.partial(local, nb=nb, nc=nc),
        mesh=mesh,
        in_specs=(
            P(("cols", "blk"), None, None),
            P(("cols", "blk"), None, None),
            P(None, None, "blk", "cols"),
            P(),
            P(),
            P(),
        ),
        out_specs=P(("cols", "blk"), None, None),
        check_vma=False,
    )
```

```python
import functools
import math

import jax
import jax.numpy as jnp
from jax import lax
from jax.experimental import pallas as pl
from jax.experimental.pallas import tpu as pltpu
from jax.sharding import PartitionSpec as P

LINE = 76
MESH = pl.DeviceIdType.MESH
F32 = jnp.float32
BF16 = jnp.bfloat16


def wave_tables(frequency_bins, samples):
    times = jnp.arange(samples, dtype=jnp.int32)
    phases = frequency_bins[:, None] * times[None, :] % samples
    angles = phases.astype(jnp.float32) * (2.0 * math.pi / samples)
    inverse = jnp.stack([jnp.cos(angles), -jnp.sin(angles)], axis=1).reshape(-1, samples)
    return inverse


def split(value):
    upper = value.astype(BF16).astype(F32)
    return upper, value - upper


def pieces_of(columns):
    width = 512
    starts = list(range(0, columns, width))
    order = []
    while starts:
        order.append(starts.pop(0))
        if starts:
            order.append(starts.pop())
    return [(start, min(width, columns - start)) for start in order]


def kernel(
    nb, nc, focal, waves, block_rows, group_columns, own, chunk,
    x_hbm, k_hbm, inv_ref, onset_ref, out_ref,
    xbuf, stage, upper, lower, spec, mix_ref, ag, table, wide, right, up_send, up_recv, mins, left, adj_recv,
    x_sem, k_sem, ag_s, ag_r, up_s, up_r, mi_s, mi_r, ad_s, ad_r,
):
    b = lax.axis_index("blk")
    c = lax.axis_index("cols")
    lines = own // LINE
    lane_tiles = xbuf.shape[1]
    half = 2 * focal
    rows = waves * half
    slots, room = stage.shape[0], xbuf.shape[0]
    chunks = k_hbm.shape[0] // chunk

    def x_copy(line, tile):
        return pltpu.make_async_copy(
            x_hbm.at[pl.ds(line * LINE * focal, LINE * focal), pl.ds(tile * 128, 128)],
            xbuf.at[line % room, tile], x_sem.at[line % room, tile],
        )

    def k_copy(index, slot):
        return pltpu.make_async_copy(
            k_hbm.at[pl.ds(pl.multiple_of(index * chunk, chunk), chunk)],
            stage.at[slot], k_sem.at[slot],
        )

    def to_blk(other):
        return {"blk": other}

    def to_cols(other):
        return {"cols": other}

    for line in range(room):
        for tile in range(lane_tiles):
            x_copy(line, tile).start()
    for slot in range(slots):
        k_copy(slot, slot).start()

    barrier = pltpu.get_barrier_semaphore()
    for d in range(1, nb):
        pl.semaphore_signal(barrier, inc=1, device_id=to_blk(lax.rem(b + d, nb)), device_id_type=MESH)
    for d in range(1, nc):
        pl.semaphore_signal(barrier, inc=1, device_id=to_cols(lax.rem(c + d, nc)), device_id_type=MESH)
    pl.semaphore_wait(barrier, nb + nc - 2)

    fwd = jnp.concatenate(split(inv_ref[...] / math.sqrt(inv_ref.shape[1])), axis=0).astype(BF16)
    for line in range(lines):
        for tile in range(lane_tiles):
            x_copy(line, tile).wait()
        for f in range(focal):
            x = jnp.concatenate(
                [xbuf.at[line % room, tile][pl.ds(f, LINE, stride=focal), :] for tile in range(lane_tiles)], axis=1
            )
            x_upper = x.astype(BF16)
            x_lower = (x - x_upper.astype(F32)).astype(BF16)
            dims = (((1,), (1,)), ((), ()))
            both = lax.dot_general(fwd, x_upper, dims, preferred_element_type=F32)
            both += lax.dot_general(fwd, x_lower, dims, preferred_element_type=F32)
            both = both[: both.shape[0] // 2] + both[both.shape[0] // 2 :]
            for j in range(2 * waves):
                spec[line, j * focal + f : j * focal + f + 1, :] = both[j : j + 1, :]
        if line + room < lines:
            for tile in range(lane_tiles):
                x_copy(line + room, tile).start()
    for line in range(lines):
        ag[b, :, line * LINE : (line + 1) * LINE] = spec[line]

    partner = b + 1 - 2 * lax.rem(b, 2)
    pairs = nb // 2

    def ag_copy(d):
        return pltpu.make_async_remote_copy(
            src_ref=ag.at[b], dst_ref=ag.at[b], send_sem=ag_s.at[d], recv_sem=ag_r.at[d],
            device_id=to_blk(lax.rem(b + 2 * d, nb) if d else partner), device_id_type=MESH,
        )

    def ag_pass(d):
        source = lax.rem(b - 2 * d + nb, nb)
        return pltpu.make_async_remote_copy(
            src_ref=ag.at[source], dst_ref=ag.at[source], send_sem=ag_s.at[pairs + d], recv_sem=ag_r.at[pairs + d],
            device_id=to_blk(partner), device_id_type=MESH,
        )

    for d in list(range(1, pairs)) + [0]:
        ag_copy(d).start()

    def take(index):
        slot = lax.rem(index, slots)
        k_copy(index, slot).wait()
        value = stage[slot]
        value_upper = value.astype(BF16)
        place = pl.ds(pl.multiple_of(index * chunk, chunk), chunk)
        upper[place, :] = value_upper
        lower[place, :] = (value - value_upper.astype(F32)).astype(BF16)

        @pl.when(index + slots < chunks)
        def _():
            k_copy(index + slots, slot).start()

    bounds = [0] + [chunks * (d + 1) // (pairs + 2) for d in range(1, pairs)] + [chunks]
    for d in range(1, pairs + 1):
        pl.loop(bounds[d - 1], bounds[d])(take)
        if d < pairs:
            ag_copy(d).wait_recv()
            ag_pass(d).start()

    samples = inv_ref.shape[1]
    times = lax.broadcasted_iota(jnp.int32, (focal, samples), 1)
    for line in range(lines):
        onset = onset_ref[line]
        window = (times < onset) | (times >= samples - onset)
        for k in range(2 * waves):
            for j in range(k, 2 * waves):
                product = inv_ref[k : k + 1, :] * (inv_ref[j : j + 1, :] / math.sqrt(samples))
                value = jnp.sum(jnp.where(window, product, 0.0), axis=1, keepdims=True)
                value = jnp.broadcast_to(value, (focal, LINE))
                for at in ((k, j), (j, k)) if j > k else ((k, j),):
                    first = (at[0] * 2 * waves + at[1]) * focal
                    mix_ref[first : first + focal, line * LINE : (line + 1) * LINE] = value

    ag_copy(0).wait()
    for d in range(1, pairs):
        ag_copy(d).wait_send()
        ag_pass(d).wait()
    for other in range(nb):
        wide[:, other * own : (other + 1) * own] = ag[other]

    def operands(value, signs):
        out = []
        for p in range(2):
            stacked = []
            for w in range(waves):
                real = value[w * half : w * half + focal]
                imag = value[w * half + focal : (w + 1) * half]
                pair = [real, imag] if p == 0 else ([-imag, real] if signs else [imag, -real])
                stacked += list(split(jnp.concatenate(pair, axis=0)))
            out.append(jnp.concatenate(stacked, axis=0))
        return out

    for tile in range(group_columns // 128):
        place = slice(tile * 128, (tile + 1) * 128)
        for p, value in enumerate(operands(wide[:, place], True)):
            right[p, place, :] = value.T.astype(BF16)

    def forward_rows(start, count):
        found = []
        for w in range(waves):
            total = None
            for p in range(2):
                place = pl.ds((w * 2 + p) * block_rows + start, count)
                if not isinstance(start, int):
                    place = pl.ds(pl.multiple_of((w * 2 + p) * block_rows + start, 16), count)
                for part in (upper, lower):
                    term = jnp.dot(part[place, :], right[p], preferred_element_type=F32)
                    total = term if total is None else total + term
            turned = total.T
            first = turned[2 * w * half : (2 * w + 1) * half]
            found.append(first + turned[(2 * w + 1) * half : (2 * w + 2) * half])
        return found

    def up_copy(d):
        other = lax.rem(c + d, nc)
        return pltpu.make_async_remote_copy(
            src_ref=up_send.at[other], dst_ref=up_recv.at[d], send_sem=up_s.at[d], recv_sem=up_r.at[d],
            device_id=to_cols(other), device_id_type=MESH,
        )

    if own % 16 == 0:
        for d in list(range(1, nc)) + [0]:
            other = lax.rem(c + d, nc)
            for w, value in enumerate(forward_rows(other * own, own)):
                up_send[other, w * half : (w + 1) * half, :] = value
            if d:
                up_copy(d).start()
    else:
        for w, value in enumerate(forward_rows(0, block_rows)):
            for other in range(nc):
                up_send[other, w * half : (w + 1) * half, :] = value[:, other * own : (other + 1) * own]
        for d in range(1, nc):
            up_copy(d).start()
    share = up_send[c]
    for d in range(1, nc):
        up_copy(d).wait()
        share = share + up_recv[d]

    for k in range(2 * waves):
        total = None
        for j in range(2 * waves):
            at = (k * 2 * waves + j) * focal
            term = mix_ref[at : at + focal, :] * share[j * focal : (j + 1) * focal]
            total = term if total is None else total + term
        mins[c, k * focal : (k + 1) * focal, :] = total

    def mi_copy(d):
        return pltpu.make_async_remote_copy(
            src_ref=mins.at[c], dst_ref=mins.at[c], send_sem=mi_s.at[d], recv_sem=mi_r.at[d],
            device_id=to_cols(lax.rem(c + d, nc)), device_id_type=MESH,
        )

    for d in range(1, nc):
        mi_copy(d).start()
    for d in range(1, nc):
        mi_copy(d).wait()
    for other in range(nc):
        table[:, other * own : (other + 1) * own] = mins[other]
    for p, value in enumerate(operands(table[...], False)):
        left[p] = value.astype(BF16)

    def ad_copy(other):
        d = lax.rem(other - b + nb, nb)
        return pltpu.make_async_remote_copy(
            src_ref=ag.at[other], dst_ref=adj_recv.at[d], send_sem=ad_s.at[d], recv_sem=ad_r.at[d],
            device_id=to_blk(other), device_id_type=MESH,
        )

    done = [False] * group_columns
    sent = set()
    for start, width in pieces_of(group_columns):
        place = slice(start, start + width)
        for w in range(waves):
            total = None
            for p in range(2):
                lhs = left[p, 2 * w * half : (2 * w + 2) * half, :]
                span = slice((w * 2 + p) * block_rows, (w * 2 + p + 1) * block_rows)
                for part in (upper, lower):
                    term = jnp.dot(lhs, part[span, place], preferred_element_type=F32)
                    total = term if total is None else total + term
            wide[w * half : (w + 1) * half, place] = total[:half] + total[half:]
        done[start : start + width] = [True] * width
        for other in range(nb):
            if other not in sent and all(done[other * own : (other + 1) * own]):
                sent.add(other)
                ag[other] = wide[:, other * own : (other + 1) * own]

                @pl.when(b != other)
                def _(other=other):
                    ad_copy(other).start()

    total = ag[b]
    for d in range(1, nb):
        ad_copy(lax.rem(b + d, nb)).wait()
        total = total + adj_recv[d]
    out_ref[...] = total


def products(spectral, kernel_rows, inverse, onsets, nb, nc, focal, waves, own):
    group_columns = kernel_rows.shape[1]
    block_rows = kernel_rows.shape[0] // (2 * waves)
    samples = spectral.shape[1]
    rows = 2 * waves * focal
    chunk = next(size for size in (64, 32, 16, 8) if kernel_rows.shape[0] % size == 0)
    lines, tiles, slots = own // LINE, samples // 128, 4
    dma = pltpu.SemaphoreType.DMA
    moved = 4 * (spectral.size + kernel_rows.size)
    return pl.pallas_call(
        functools.partial(kernel, nb, nc, focal, waves, block_rows, group_columns, own, chunk),
        out_shape=jax.ShapeDtypeStruct((rows, own), F32),
        in_specs=[pl.BlockSpec(memory_space=pl.ANY)] * 2 + [pl.BlockSpec(memory_space=pltpu.VMEM)] * 2,
        out_specs=pl.BlockSpec(memory_space=pltpu.VMEM),
        scratch_shapes=[
            pltpu.VMEM((min(lines, 3), tiles, LINE * focal, 128), F32),
            pltpu.VMEM((slots, chunk, group_columns), F32),
            pltpu.VMEM(kernel_rows.shape, BF16),
            pltpu.VMEM(kernel_rows.shape, BF16),
            pltpu.VMEM((lines, rows, LINE), F32),
            pltpu.VMEM((2 * waves * rows, own), F32),
            pltpu.VMEM((nb, rows, own), F32),
            pltpu.VMEM((rows, block_rows), F32),
            pltpu.VMEM((rows, group_columns), F32),
            pltpu.VMEM((2, group_columns, 2 * rows), BF16),
            pltpu.VMEM((nc, rows, own), F32),
            pltpu.VMEM((nc, rows, own), F32),
            pltpu.VMEM((nc, rows, own), F32),
            pltpu.VMEM((2, 2 * rows, block_rows), BF16),
            pltpu.VMEM((nb, rows, own), F32),
            dma((min(lines, 3), tiles)), dma((slots,)),
            dma((nb,)), dma((nb,)), dma((nc,)), dma((nc,)), dma((nc,)), dma((nc,)), dma((nb,)), dma((nb,)),
        ],
        compiler_params=pltpu.CompilerParams(
            collective_id=0, has_side_effects=True, vmem_limit_bytes=63 << 20
        ),
        cost_estimate=pl.CostEstimate(
            flops=16 * kernel_rows.size * focal, bytes_accessed=moved, transcendentals=0
        ),
    )(spectral, kernel_rows, inverse, onsets)


def final(update_ref, inv_ref, onset_ref, direct_ref, out_ref):
    focal, samples = onset_ref.shape[1], inv_ref.shape[1]
    value = update_ref[0]
    value = jnp.concatenate([value, jnp.zeros((8 - value.shape[0], value.shape[1]), F32)], axis=0)
    upper, lower = split(value)
    inv_upper, inv_lower = split(inv_ref[...])
    lhs = jnp.concatenate([upper, upper, lower, lower], axis=0).T.astype(BF16)
    rhs = jnp.concatenate([inv_upper, inv_lower, inv_upper, inv_lower], axis=0).astype(BF16)
    correction = jnp.dot(lhs, rhs, preferred_element_type=F32).reshape(-1, focal, samples)
    onset = onset_ref[0]
    times = lax.broadcasted_iota(jnp.int32, (focal, samples), 1)
    window = (times < onset) | (times >= samples - onset)
    out_ref[...] = direct_ref[...] - jnp.where(window[None], correction, 0.0)


def local(focusing_plus, direct_field, reflectivity, frequency_bins, focal_onsets, line_offsets, nb, nc):
    own, focal, samples = focusing_plus.shape
    waves, _, block_rows, group_columns = reflectivity.shape
    lines = own // LINE
    inverse = wave_tables(frequency_bins, samples)
    inverse = jnp.pad(inverse, ((0, 8 - 2 * waves), (0, 0)))
    block_index = lax.axis_index("blk")
    group_index = lax.axis_index("cols")

    def onsets_from(first):
        offsets = lax.dynamic_slice_in_dim(line_offsets, first // LINE, lines)
        return (focal_onsets[None, :] + offsets[:, None])[:, :, None]

    share_onsets = onsets_from(block_index * block_rows + group_index * own)
    source_onsets = onsets_from(group_index * group_columns + block_index * own)
    update = products(
        focusing_plus.reshape(own * focal, samples), reflectivity.reshape(-1, group_columns),
        inverse, share_onsets, nb, nc, focal, waves, own,
    )
    update = update.reshape(2 * waves, focal, lines, LINE).transpose(2, 0, 3, 1)
    update = update.reshape(lines, 2 * waves, LINE * focal)
    block = pl.BlockSpec((LINE, focal, samples), lambda i: (i, 0, 0))
    return pl.pallas_call(
        final,
        grid=(lines,),
        out_shape=jax.ShapeDtypeStruct(direct_field.shape, F32),
        in_specs=[
            pl.BlockSpec((1, 2 * waves, LINE * focal), lambda i: (i, 0, 0)),
            pl.BlockSpec(inverse.shape, lambda i: (0, 0)),
            pl.BlockSpec((1, focal, 1), lambda i: (i, 0, 0)),
            block,
        ],
        out_specs=block,
        compiler_params=pltpu.CompilerParams(vmem_limit_bytes=48 << 20),
    )(update, inverse, source_onsets, direct_field)


def solution(mesh):
    nb, nc = mesh.shape["blk"], mesh.shape["cols"]
    return jax.shard_map(
        functools.partial(local, nb=nb, nc=nc),
        mesh=mesh,
        in_specs=(
            P(("cols", "blk"), None, None),
            P(("cols", "blk"), None, None),
            P(None, None, "blk", "cols"),
            P(),
            P(),
            P(),
        ),
        out_specs=P(("cols", "blk"), None, None),
        check_vma=False,
    )
```
